32 devices in a mesh: dp: 4 (over y, x), fsdp: 8 (over z, core).
Axes of the slice: x: 2, y: 2, z: 4, core: 2. Of those that a mesh axis runs over, the one named last changes fastest.
Arguments:
- states: bfloat16 [8192, 8192], P(('dp', 'fsdp')), may hold values from -6 to 6
- queries: bfloat16 [8192, 4096], P(('dp', 'fsdp')), may hold values from -5 to 5
- keys: bfloat16 [8192, 1024], P(('dp', 'fsdp')), may hold values from -5 to 5
- dest_device: int32 [8192], P(('dp', 'fsdp')), may hold values from 0 to 31, as said below
- dest_offset: int32 [8192], P(('dp', 'fsdp')), may hold values from 0 to 255, as said below
- response_numbers: int32 [8192], P(('dp', 'fsdp')), may hold values from 0 to 3, as said below
- cotangent: bfloat16 [8192, 4096], P(('dp', 'fsdp')), may hold values from -6 to 6
- value_matrix: bfloat16 [8192, 1024], P('fsdp'), may hold values from -0.0625 to 0.0625
Outputs:
- attn_out: bfloat16 [8192, 4096], P(('dp', 'fsdp'))
- grad_query: bfloat16 [8192, 4096], P(('dp', 'fsdp'))
- grad_key: bfloat16 [8192, 1024], P(('dp', 'fsdp'))
- grad_value_weight: float32 [8192, 1024], P('fsdp')
The draws below stay inside these ranges and needn't reach their ends.
Inputs may be any that keep to these rules, and one draw needn't show every extreme that they name: `dest_device`: each device sends exactly 8 rows to each of 32 different devices, and every device receives exactly 256 rows. `dest_offset`: the rows that one device receives have different offsets. `response_numbers`: each device's 256 rows hold exactly 4 responses in order: ids start at 0 on each device and never fall along its rows.
All inputs are finite; a program needn't handle non-finite values.
Results may differ from the reference program's by a relative error of at most 0.017.
Values may be sent and summed in bfloat16 or wider, within the bound.
A program may use at most 192 MiB of HBM per device.

```python
import math
import jax
import jax.numpy as jnp
from jax import lax

MODEL_WIDTH = 8192
KEY_VALUE_HEADS = 8
HEAD_SIZE = 128
QUERY_HEADS = 32
DEVICE_TOKENS = 256
DOCS = 4
CAP = 8
TOTAL_TOKENS = 8192
N_DP = 4
N_FSDP = 8


def plan_tables(key):
    device_count = N_DP * N_FSDP
    dest_count = DEVICE_TOKENS // CAP
    half_way = device_count // 2
    first_key, second_key, third_key = jax.random.split(jax.random.fold_in(key, 7), 3)
    remaining = jax.random.permutation(first_key, device_count - 1).astype(jnp.int32)
    remaining = remaining + (remaining >= half_way).astype(jnp.int32)
    shifts = jnp.concatenate([jnp.full((1,), half_way, jnp.int32), remaining])[:dest_count]
    row_order = jax.vmap(lambda inner: jax.random.permutation(inner, DEVICE_TOKENS))(jax.random.split(second_key, device_count))
    permuted = jax.vmap(lambda inner: jax.random.permutation(inner, DEVICE_TOKENS))(jax.random.split(third_key, device_count))
    source = jnp.arange(device_count, dtype=jnp.int32)[:, None]
    dest_rank = row_order // CAP
    target = (source + shifts[dest_rank]) % device_count
    offsets = permuted[target, row_order]
    return (target.reshape(TOTAL_TOKENS).astype(jnp.int32), offsets.reshape(TOTAL_TOKENS).astype(jnp.int32))


def draw_dest_device(key, part):
    return plan_tables(key)[0]


def draw_dest_offset(key, part):
    return plan_tables(key)[1]


def draw_response_numbers(key, part):
    device_count = N_DP * N_FSDP
    keys_all = jax.random.split(jax.random.fold_in(key, 13), device_count)

    def one_device(inner):
        cuts = (jax.random.permutation(inner, DEVICE_TOKENS - 1) + 1)[:DOCS - 1]
        position = jnp.arange(DEVICE_TOKENS, dtype=jnp.int32)
        return jnp.sum((cuts[None, :] <= position[:, None]).astype(jnp.int32), axis=1)
    return jax.vmap(one_device)(keys_all).reshape(TOTAL_TOKENS).astype(jnp.int32)


def query_key(key):
    query_seed, random_key_seed = jax.random.split(jax.random.fold_in(key, 11), 2)
    query_vals = jnp.clip(jax.random.normal(query_seed, (TOTAL_TOKENS, QUERY_HEADS * HEAD_SIZE), jnp.float32), -5.0, 5.0)
    key_value_rows = jnp.clip(jax.random.normal(random_key_seed, (TOTAL_TOKENS, KEY_VALUE_HEADS * HEAD_SIZE), jnp.float32), -5.0, 5.0)
    return (query_vals, key_value_rows)


def draw_queries(key, part):
    return query_key(key)[0].astype(jnp.bfloat16)


def draw_keys(key, part):
    return query_key(key)[1].astype(jnp.bfloat16)


def levels(own_key, shape, cuts, low, top_value):
    def one(dim, parts):
        draws = jax.random.uniform(jax.random.fold_in(jax.random.fold_in(own_key, 6), dim), (parts,), jnp.float32, low / len(cuts), top_value / len(cuts))
        return jnp.repeat(jnp.exp(draws), shape[dim] // parts).reshape((-1,) + (1,) * (len(shape) - dim - 1))

    loudness = one(*cuts[0])
    for cut in cuts[1:]:
        loudness = loudness * one(*cut)
    return loudness


def noise(stream_key, extent, scale, limit, cuts=(), kind=jnp.bfloat16):
    loudness = levels(stream_key, extent, cuts, -0.22, 0.18) if cuts else 1.0
    drawn = jax.random.normal(stream_key, extent, jnp.float32) * scale * loudness
    return jnp.minimum(jnp.maximum(drawn, -limit), limit).astype(kind)


def setup_inputs(seed: int = 0) -> dict:
    key_of = jax.random.split(jax.random.key(seed), 9)
    states = noise(key_of[0], (TOTAL_TOKENS, MODEL_WIDTH), 1.0, 6.0, ((0, 32),))
    queries = draw_queries(jax.random.fold_in(key_of[8], 71), 0)
    keys = draw_keys(jax.random.fold_in(key_of[8], 71), 0)
    dest_device = draw_dest_device(jax.random.fold_in(key_of[8], 71), 0)
    dest_offset = draw_dest_offset(jax.random.fold_in(key_of[8], 71), 0)
    response_numbers = draw_response_numbers(jax.random.fold_in(key_of[8], 71), 0)
    cotangent = noise(key_of[6], (TOTAL_TOKENS, QUERY_HEADS * HEAD_SIZE), 1.0, 6.0, ((0, 32),))
    value_matrix = noise(key_of[7], (MODEL_WIDTH, KEY_VALUE_HEADS * HEAD_SIZE), MODEL_WIDTH ** -0.5, 0.0625, ((0, 8),))
    return {"states": states, "queries": queries, "keys": keys, "dest_device": dest_device, "dest_offset": dest_offset, "response_numbers": response_numbers, "cotangent": cotangent, "value_matrix": value_matrix}


def attend_block(block_query_rows, block_key_rows, block_value_rows, block_segments, block_upstream_grad):
    token_count = block_query_rows.shape[0]
    head_group = QUERY_HEADS // KEY_VALUE_HEADS
    inverse = 1.0 / math.sqrt(HEAD_SIZE)
    query_head_rows = block_query_rows.astype(jnp.float32).reshape(token_count, KEY_VALUE_HEADS, head_group, HEAD_SIZE)
    key_head_rows = block_key_rows.astype(jnp.float32).reshape(token_count, KEY_VALUE_HEADS, HEAD_SIZE)
    value_head_rows = block_value_rows.astype(jnp.float32).reshape(token_count, KEY_VALUE_HEADS, HEAD_SIZE)
    output_gradient = block_upstream_grad.astype(jnp.float32).reshape(token_count, KEY_VALUE_HEADS, head_group, HEAD_SIZE)
    scores = jnp.einsum('tkgd,skd->kgts', query_head_rows, key_head_rows) * inverse
    position = jnp.arange(token_count, dtype=jnp.int32)
    allowed = (position[None, :] <= position[:, None]) & (block_segments[None, :] == block_segments[:, None])
    scores = jnp.where(allowed, scores, -1e+30)
    highest = lax.optimization_barrier(jnp.max(scores, axis=-1, keepdims=True))
    expon = jnp.exp(scores - highest)
    probs = expon / lax.optimization_barrier(jnp.sum(expon, axis=-1, keepdims=True))
    probs_low = lax.optimization_barrier(probs.astype(jnp.bfloat16)).astype(jnp.float32)
    attention_fn = jnp.einsum('kgts,skd->tkgd', probs_low, value_head_rows).astype(jnp.bfloat16)
    dprobs = jnp.einsum('tkgd,skd->kgts', output_gradient, value_head_rows)
    delta = lax.optimization_barrier(jnp.sum(probs * dprobs, axis=-1, keepdims=True))
    dscores = lax.optimization_barrier((probs * (dprobs - delta)).astype(jnp.bfloat16)).astype(jnp.float32)
    query_gradient = (jnp.einsum('kgts,skd->tkgd', dscores, key_head_rows) * inverse).astype(jnp.bfloat16)
    key_gradient = (jnp.einsum('kgts,tkgd->skd', dscores, query_head_rows) * inverse).astype(jnp.bfloat16)
    value_gradient = jnp.einsum('kgts,tkgd->skd', probs_low, output_gradient).astype(jnp.bfloat16)
    return (attention_fn.reshape(token_count, QUERY_HEADS * HEAD_SIZE), query_gradient.reshape(token_count, QUERY_HEADS * HEAD_SIZE), key_gradient.reshape(token_count, KEY_VALUE_HEADS * HEAD_SIZE), value_gradient.reshape(token_count, KEY_VALUE_HEADS * HEAD_SIZE))

def reference(states, queries, keys, dest_device, dest_offset, response_numbers, cotangent, value_matrix):
    device_count = N_DP * N_FSDP
    place = (dest_device * DEVICE_TOKENS + dest_offset).astype(jnp.int32)
    trainer_states = jnp.zeros_like(states).at[place].set(states)
    trainer_queries = jnp.zeros_like(queries).at[place].set(queries)
    trainer_keys = jnp.zeros_like(keys).at[place].set(keys)

    def one_device(running_total, input_rows):
        block_states, block_query_rows, block_key_rows, block_segments, block_upstream_grad = input_rows
        values = jnp.dot(block_states, value_matrix, preferred_element_type=jnp.float32).astype(jnp.bfloat16)
        attention_fn, query_gradient, key_gradient, value_gradient = attend_block(block_query_rows, block_key_rows, values, block_segments, block_upstream_grad)
        partial_term = lax.dot_general(block_states, value_gradient, (((0,), (0,)), ((), ())), preferred_element_type=jnp.float32).astype(jnp.bfloat16)
        partial_term = lax.optimization_barrier(partial_term)
        return (running_total + partial_term.astype(jnp.float32), (attention_fn, query_gradient, key_gradient))
    starting_total = jnp.zeros((MODEL_WIDTH, KEY_VALUE_HEADS * HEAD_SIZE), jnp.float32)
    input_rows = (trainer_states.reshape(device_count, DEVICE_TOKENS, MODEL_WIDTH), trainer_queries.reshape(device_count, DEVICE_TOKENS, QUERY_HEADS * HEAD_SIZE), trainer_keys.reshape(device_count, DEVICE_TOKENS, KEY_VALUE_HEADS * HEAD_SIZE), response_numbers.reshape(device_count, DEVICE_TOKENS), cotangent.reshape(device_count, DEVICE_TOKENS, QUERY_HEADS * HEAD_SIZE))
    running_total, outputs = lax.scan(one_device, starting_total, input_rows)
    attention_fn, query_gradient, key_gradient = outputs
    score_scale = 1.0 / math.sqrt(TOTAL_TOKENS)
    return (attention_fn.reshape(TOTAL_TOKENS, QUERY_HEADS * HEAD_SIZE), query_gradient.reshape(TOTAL_TOKENS, QUERY_HEADS * HEAD_SIZE), key_gradient.reshape(TOTAL_TOKENS, KEY_VALUE_HEADS * HEAD_SIZE), running_total * score_scale)
```

```python
import math

import jax
import jax.numpy as jnp
from jax import lax
from jax.sharding import PartitionSpec as P

KEY_VALUE_HEADS = 8
HEAD_SIZE = 128
QUERY_HEADS = 32


def attend_block(
    block_query_rows, block_key_rows, block_value_rows, block_segments, block_upstream_grad
):
    token_count = block_query_rows.shape[0]
    head_group = QUERY_HEADS // KEY_VALUE_HEADS
    inverse = 1.0 / math.sqrt(HEAD_SIZE)
    query_head_rows = block_query_rows.reshape(token_count, KEY_VALUE_HEADS, head_group, HEAD_SIZE)
    key_head_rows = block_key_rows.reshape(token_count, KEY_VALUE_HEADS, HEAD_SIZE)
    value_head_rows = block_value_rows.reshape(token_count, KEY_VALUE_HEADS, HEAD_SIZE)
    output_gradient = block_upstream_grad.reshape(
        token_count, KEY_VALUE_HEADS, head_group, HEAD_SIZE
    )
    scores = (
        jnp.einsum(
            "tkgd,skd->kgts", query_head_rows, key_head_rows, preferred_element_type=jnp.float32
        )
        * inverse
    )
    position = jnp.arange(token_count, dtype=jnp.int32)
    allowed = (position[None, :] <= position[:, None]) & (
        block_segments[None, :] == block_segments[:, None]
    )
    scores = jnp.where(allowed, scores, -1e30)
    highest = jnp.max(scores, axis=-1, keepdims=True)
    expon = jnp.exp(scores - highest)
    probs = expon / jnp.sum(expon, axis=-1, keepdims=True)
    probs_low = probs.astype(jnp.bfloat16)
    attention_fn = jnp.einsum(
        "kgts,skd->tkgd", probs_low, value_head_rows, preferred_element_type=jnp.float32
    ).astype(jnp.bfloat16)
    dprobs = jnp.einsum(
        "tkgd,skd->kgts", output_gradient, value_head_rows, preferred_element_type=jnp.float32
    )
    delta = jnp.sum(probs * dprobs, axis=-1, keepdims=True)
    dscores = (probs * (dprobs - delta)).astype(jnp.bfloat16)
    query_gradient = (
        jnp.einsum("kgts,skd->tkgd", dscores, key_head_rows, preferred_element_type=jnp.float32)
        * inverse
    ).astype(jnp.bfloat16)
    key_gradient = (
        jnp.einsum("kgts,tkgd->skd", dscores, query_head_rows, preferred_element_type=jnp.float32)
        * inverse
    ).astype(jnp.bfloat16)
    value_gradient = jnp.einsum(
        "kgts,tkgd->skd", probs_low, output_gradient, preferred_element_type=jnp.float32
    ).astype(jnp.bfloat16)
    return (
        attention_fn.reshape(token_count, QUERY_HEADS * HEAD_SIZE),
        query_gradient.reshape(token_count, QUERY_HEADS * HEAD_SIZE),
        key_gradient.reshape(token_count, KEY_VALUE_HEADS * HEAD_SIZE),
        value_gradient.reshape(token_count, KEY_VALUE_HEADS * HEAD_SIZE),
    )


def ordered_dot(one_hot, rows):
    return jnp.dot(one_hot, rows, preferred_element_type=jnp.float32).astype(rows.dtype)


def per_device(
    states, queries, keys, dest_device, dest_offset, response_numbers, cotangent, value_matrix
):
    token_count, model_width = states.shape
    group_dp = lax.axis_size("dp")
    group_fsdp = lax.axis_size("fsdp")
    device_count = group_dp * group_fsdp
    capacity = token_count // device_count
    everyone = ("dp", "fsdp")
    low = states.dtype
    share = value_matrix.shape[0] // group_dp
    own_share = lax.dynamic_slice_in_dim(value_matrix, lax.axis_index("dp") * share, share, 0)
    whole = lax.all_gather(own_share, everyone, axis=0)

    row = jnp.arange(token_count, dtype=jnp.int32)
    earlier = (dest_device[:, None] == dest_device[None, :]) & (row[None, :] < row[:, None])
    slot = jnp.sum(earlier.astype(jnp.int32), axis=1)
    index = dest_device * capacity + slot
    pack = (index[None, :] == row[:, None]).astype(low)
    tail = jnp.broadcast_to(dest_offset.astype(low)[:, None], (token_count, 128))
    joined = jnp.concatenate([queries, keys, tail], axis=1)

    def exchange(rows):
        width = rows.shape[1]
        moved = lax.all_to_all(
            rows.reshape(device_count, capacity, width),
            everyone,
            split_axis=0,
            concat_axis=0,
            tiled=True,
        )
        return moved.reshape(token_count, width)

    got = exchange(ordered_dot(pack, joined))
    whole = whole.reshape(group_dp, group_fsdp, share, -1).transpose(1, 0, 2, 3)
    whole = whole.reshape(model_width, -1)
    values = jnp.dot(states, whole, preferred_element_type=jnp.float32).astype(low)
    got_values = exchange(ordered_dot(pack, values))
    target = got[:, -128].astype(jnp.int32)
    place = (target[None, :] == row[:, None]).astype(low)
    query_width = queries.shape[1]
    placed = ordered_dot(place, got)
    learner_queries = placed[:, :query_width]
    learner_keys = placed[:, query_width : query_width + keys.shape[1]]
    attention_fn, query_gradient, key_gradient, value_gradient = attend_block(
        learner_queries, learner_keys, ordered_dot(place, got_values), response_numbers, cotangent
    )
    returned = exchange(ordered_dot(place.T, value_gradient))
    row_grads = ordered_dot(pack.T, returned)
    term = lax.dot_general(
        states, row_grads, (((0,), (0,)), ((), ())), preferred_element_type=jnp.float32
    ).astype(low)
    width = term.shape[1]
    term = term.reshape(group_fsdp, group_dp, share, width).transpose(1, 0, 2, 3)
    term = term.reshape(model_width, width)
    owned = lax.psum_scatter(term, everyone, scatter_dimension=0, tiled=True)
    summed = lax.all_gather(owned, "dp", axis=0, tiled=True).astype(jnp.float32)
    score_scale = 1.0 / math.sqrt(token_count * device_count)
    return (attention_fn, query_gradient, key_gradient, summed * score_scale)


def solution(mesh):
    in_specs = (
        P(("dp", "fsdp"), None),
        P(("dp", "fsdp"), None),
        P(("dp", "fsdp"), None),
        P(("dp", "fsdp")),
        P(("dp", "fsdp")),
        P(("dp", "fsdp")),
        P(("dp", "fsdp"), None),
        P("fsdp", None),
    )
    out_specs = (
        P(("dp", "fsdp"), None),
        P(("dp", "fsdp"), None),
        P(("dp", "fsdp"), None),
        P("fsdp", None),
    )
    return jax.shard_map(
        per_device, mesh=mesh, in_specs=in_specs, out_specs=out_specs, check_vma=False
    )
```

```python
import math

import jax
import jax.numpy as jnp
from jax import lax
from jax.experimental import pallas as pl
from jax.sharding import PartitionSpec as P

KEY_VALUE_HEADS = 8
HEAD_SIZE = 128
QUERY_HEADS = 32


def attend_kernel(q_ref, k_ref, v_ref, g_ref, col_ref, row_ref, o_ref, dq_ref, dk_ref, dv_ref):
    token_count = k_ref.shape[0]
    inverse = 1.0 / math.sqrt(HEAD_SIZE)
    low = q_ref.dtype
    query_at = lax.broadcasted_iota(jnp.int32, (token_count, token_count), 0)
    key_at = lax.broadcasted_iota(jnp.int32, (token_count, token_count), 1)
    allowed = (key_at <= query_at) & (row_ref[...] == col_ref[...])
    k = k_ref[...]
    v = v_ref[...]

    def dot(x, y, dims):
        return lax.dot_general(x, y, (dims, ((), ())), preferred_element_type=jnp.float32)

    for head in range(QUERY_HEADS // KEY_VALUE_HEADS):
        part = slice(head * HEAD_SIZE, (head + 1) * HEAD_SIZE)
        q = q_ref[:, part]
        g = g_ref[:, part]
        scores = jnp.where(allowed, dot(q, k, ((1,), (1,))) * inverse, -1e30)
        expon = jnp.exp(scores - jnp.max(scores, axis=1, keepdims=True))
        probs = expon * (1.0 / jnp.sum(expon, axis=1, keepdims=True))
        probs_low = probs.astype(low)
        o_ref[:, part] = dot(probs_low, v, ((1,), (0,))).astype(low)
        dprobs = dot(g, v, ((1,), (1,)))
        delta = jnp.sum(probs * dprobs, axis=1, keepdims=True)
        dscores = (probs * (dprobs - delta)).astype(low)
        dq_ref[:, part] = (dot(dscores, k, ((1,), (0,))) * inverse).astype(low)
        key_term = dot(dscores, q, ((0,), (0,)))
        value_term = dot(probs_low, g, ((0,), (0,)))
        dk = key_term if head == 0 else dk + key_term
        dv = value_term if head == 0 else dv + value_term
    dk_ref[...] = (dk * inverse).astype(low)
    dv_ref[...] = dv.astype(low)


def attend_block(q, k, v, segments, g):
    token_count = q.shape[0]
    wide = pl.BlockSpec((token_count, q.shape[1] // KEY_VALUE_HEADS), lambda h: (0, h))
    thin = pl.BlockSpec((token_count, HEAD_SIZE), lambda h: (0, h))
    col = pl.BlockSpec((token_count, 1), lambda h: (0, 0))
    row = pl.BlockSpec((1, token_count), lambda h: (0, 0))
    out = [jax.ShapeDtypeStruct(x.shape, q.dtype) for x in (q, q, k, k)]
    return pl.pallas_call(
        attend_kernel,
        grid=(KEY_VALUE_HEADS,),
        in_specs=[wide, thin, thin, wide, col, row],
        out_specs=[wide, wide, thin, thin],
        out_shape=out,
        cost_estimate=pl.CostEstimate(
            flops=12 * QUERY_HEADS * token_count * token_count * HEAD_SIZE,
            bytes_accessed=40 * token_count * QUERY_HEADS * HEAD_SIZE // 4,
            transcendentals=QUERY_HEADS * token_count * token_count,
        ),
    )(q, k, v, g, segments[:, None], segments[None, :])


def ordered_dot(one_hot, rows):
    return jnp.dot(one_hot, rows, preferred_element_type=jnp.float32).astype(rows.dtype)


def per_device(
    states, queries, keys, dest_device, dest_offset, response_numbers, cotangent, value_matrix
):
    token_count, model_width = states.shape
    group_dp = lax.axis_size("dp")
    group_fsdp = lax.axis_size("fsdp")
    device_count = group_dp * group_fsdp
    capacity = token_count // device_count
    everyone = ("dp", "fsdp")
    low = states.dtype
    share = value_matrix.shape[0] // group_dp
    own_share = lax.dynamic_slice_in_dim(value_matrix, lax.axis_index("dp") * share, share, 0)
    whole = lax.all_gather(own_share, everyone, axis=0)

    row = jnp.arange(token_count, dtype=jnp.int32)
    earlier = (dest_device[:, None] == dest_device[None, :]) & (row[None, :] < row[:, None])
    slot = jnp.sum(earlier.astype(jnp.int32), axis=1)
    index = dest_device * capacity + slot
    pack = (index[None, :] == row[:, None]).astype(low)
    tail = jnp.broadcast_to(dest_offset.astype(low)[:, None], (token_count, 128))
    joined = jnp.concatenate([queries, keys, tail], axis=1)

    def exchange(rows):
        width = rows.shape[1]
        moved = lax.all_to_all(
            rows.reshape(device_count, capacity, width),
            everyone,
            split_axis=0,
            concat_axis=0,
            tiled=True,
        )
        return moved.reshape(token_count, width)

    got = exchange(ordered_dot(pack, joined))
    whole = whole.reshape(group_dp, group_fsdp, share, -1).transpose(1, 0, 2, 3)
    whole = whole.reshape(model_width, -1)
    values = jnp.dot(states, whole, preferred_element_type=jnp.float32).astype(low)
    got_values = exchange(ordered_dot(pack, values))
    block = model_width // group_fsdp
    moving, got_values = lax.optimization_barrier((states, got_values))
    column_states = lax.all_to_all(
        moving.reshape(token_count, group_fsdp, block).transpose(1, 0, 2),
        "fsdp",
        split_axis=0,
        concat_axis=0,
        tiled=True,
    ).reshape(group_fsdp * token_count, block)
    target = got[:, -128].astype(jnp.int32)
    place = (target[None, :] == row[:, None]).astype(low)
    query_width = queries.shape[1]
    placed = ordered_dot(place, got)
    learner_queries = placed[:, :query_width]
    learner_keys = placed[:, query_width : query_width + keys.shape[1]]
    attention_fn, query_gradient, key_gradient, value_gradient = attend_block(
        learner_queries, learner_keys, ordered_dot(place, got_values), response_numbers, cotangent
    )
    returned = exchange(ordered_dot(place.T, value_gradient))
    row_grads = ordered_dot(pack.T, returned)
    group_grads = lax.all_gather(row_grads, "fsdp", axis=0, tiled=True)
    term = lax.dot_general(
        column_states, group_grads, (((0,), (0,)), ((), ())), preferred_element_type=jnp.float32
    ).astype(low)
    summed = lax.psum(term, "dp").astype(jnp.float32)
    score_scale = 1.0 / math.sqrt(token_count * device_count)
    return (attention_fn, query_gradient, key_gradient, summed * score_scale)


def solution(mesh):
    in_specs = (
        P(("dp", "fsdp"), None),
        P(("dp", "fsdp"), None),
        P(("dp", "fsdp"), None),
        P(("dp", "fsdp")),
        P(("dp", "fsdp")),
        P(("dp", "fsdp")),
        P(("dp", "fsdp"), None),
        P("fsdp", None),
    )
    out_specs = (
        P(("dp", "fsdp"), None),
        P(("dp", "fsdp"), None),
        P(("dp", "fsdp"), None),
        P("fsdp", None),
    )
    return jax.shard_map(
        per_device, mesh=mesh, in_specs=in_specs, out_specs=out_specs, check_vma=False
    )
```

```python
import math

import jax
import jax.numpy as jnp
from jax import lax
from jax.experimental import pallas as pl
from jax.sharding import PartitionSpec as P

KEY_VALUE_HEADS = 8
HEAD_SIZE = 128
QUERY_HEADS = 32


def attend_kernel(q_ref, k_ref, v_ref, g_ref, col_ref, row_ref, o_ref, dq_ref, dk_ref, dv_ref):
    token_count = k_ref.shape[0]
    inverse = 1.0 / math.sqrt(HEAD_SIZE)
    low = q_ref.dtype
    query_at = lax.broadcasted_iota(jnp.int32, (token_count, token_count), 0)
    key_at = lax.broadcasted_iota(jnp.int32, (token_count, token_count), 1)
    allowed = (key_at <= query_at) & (row_ref[...] == col_ref[...])
    k = k_ref[...]
    v = v_ref[...]

    def dot(x, y, dims):
        return lax.dot_general(x, y, (dims, ((), ())), preferred_element_type=jnp.float32)

    for head in range(QUERY_HEADS // KEY_VALUE_HEADS):
        part = slice(head * HEAD_SIZE, (head + 1) * HEAD_SIZE)
        q = q_ref[:, part]
        g = g_ref[:, part]
        scores = jnp.where(allowed, dot(q, k, ((1,), (1,))) * inverse, -1e30)
        expon = jnp.exp(scores - jnp.max(scores, axis=1, keepdims=True))
        probs = expon * (1.0 / jnp.sum(expon, axis=1, keepdims=True))
        probs_low = probs.astype(low)
        o_ref[:, part] = dot(probs_low, v, ((1,), (0,))).astype(low)
        dprobs = dot(g, v, ((1,), (1,)))
        delta = jnp.sum(probs * dprobs, axis=1, keepdims=True)
        dscores = (probs * (dprobs - delta)).astype(low)
        dq_ref[:, part] = (dot(dscores, k, ((1,), (0,))) * inverse).astype(low)
        key_term = dot(dscores, q, ((0,), (0,)))
        value_term = dot(probs_low, g, ((0,), (0,)))
        dk = key_term if head == 0 else dk + key_term
        dv = value_term if head == 0 else dv + value_term
    dk_ref[...] = (dk * inverse).astype(low)
    dv_ref[...] = dv.astype(low)


def attend_block(q, k, v, segments, g):
    token_count = q.shape[0]
    wide = pl.BlockSpec((token_count, q.shape[1] // KEY_VALUE_HEADS), lambda h: (0, h))
    thin = pl.BlockSpec((token_count, HEAD_SIZE), lambda h: (0, h))
    col = pl.BlockSpec((token_count, 1), lambda h: (0, 0))
    row = pl.BlockSpec((1, token_count), lambda h: (0, 0))
    out = [jax.ShapeDtypeStruct(x.shape, q.dtype) for x in (q, q, k, k)]
    return pl.pallas_call(
        attend_kernel,
        grid=(KEY_VALUE_HEADS,),
        in_specs=[wide, thin, thin, wide, col, row],
        out_specs=[wide, wide, thin, thin],
        out_shape=out,
        cost_estimate=pl.CostEstimate(
            flops=12 * QUERY_HEADS * token_count * token_count * HEAD_SIZE,
            bytes_accessed=40 * token_count * QUERY_HEADS * HEAD_SIZE // 4,
            transcendentals=QUERY_HEADS * token_count * token_count,
        ),
    )(q, k, v, g, segments[:, None], segments[None, :])


def ordered_dot(one_hot, rows):
    return jnp.dot(one_hot, rows, preferred_element_type=jnp.float32).astype(rows.dtype)


def per_device(
    states, queries, keys, dest_device, dest_offset, response_numbers, cotangent, value_matrix
):
    token_count, model_width = states.shape
    group_dp = lax.axis_size("dp")
    group_fsdp = lax.axis_size("fsdp")
    device_count = group_dp * group_fsdp
    capacity = token_count // device_count
    everyone = ("dp", "fsdp")
    low = states.dtype
    share = value_matrix.shape[0] // group_dp
    block = model_width // group_fsdp
    me = lax.axis_index("fsdp")
    blocks = []
    for step in range(group_fsdp):
        to = lax.rem(me + step, group_fsdp)
        piece = lax.dynamic_slice_in_dim(states, to * block, block, 1)
        if step:
            pairs = [(i, (i + step) % group_fsdp) for i in range(group_fsdp)]
            piece = lax.ppermute(piece, "fsdp", pairs)
        blocks.append(piece)
    own_share = lax.dynamic_slice_in_dim(value_matrix, lax.axis_index("dp") * share, share, 0)
    whole = lax.all_gather(own_share, everyone, axis=0)

    row = jnp.arange(token_count, dtype=jnp.int32)
    earlier = (dest_device[:, None] == dest_device[None, :]) & (row[None, :] < row[:, None])
    slot = jnp.sum(earlier.astype(jnp.int32), axis=1)
    index = dest_device * capacity + slot
    pack = (index[None, :] == row[:, None]).astype(low)
    tail = jnp.broadcast_to(dest_offset.astype(low)[:, None], (token_count, 128))
    joined = jnp.concatenate([queries, keys, tail], axis=1)

    def exchange(rows):
        width = rows.shape[1]
        moved = lax.all_to_all(
            rows.reshape(device_count, capacity, width),
            everyone,
            split_axis=0,
            concat_axis=0,
            tiled=True,
        )
        return moved.reshape(token_count, width)

    got = exchange(ordered_dot(pack, joined))
    turned = states.reshape(token_count, group_fsdp, group_dp, share).transpose(0, 2, 1, 3)
    turned = turned.reshape(token_count, model_width)
    values = jnp.dot(turned, whole.reshape(model_width, -1), preferred_element_type=jnp.float32).astype(low)
    got_values = exchange(ordered_dot(pack, values))
    target = got[:, -128].astype(jnp.int32)
    place = (target[None, :] == row[:, None]).astype(low)
    query_width = queries.shape[1]
    placed = ordered_dot(place, got)
    learner_queries = placed[:, :query_width]
    learner_keys = placed[:, query_width : query_width + keys.shape[1]]
    attention_fn, query_gradient, key_gradient, value_gradient = attend_block(
        learner_queries, learner_keys, ordered_dot(place, got_values), response_numbers, cotangent
    )
    back = [blocks[-t % group_fsdp] for t in range(group_fsdp)]
    first = lax.rem(group_fsdp - me, group_fsdp) * token_count
    column_states = lax.dynamic_slice_in_dim(
        jnp.concatenate(back + back[:-1], axis=0), first, group_fsdp * token_count, 0
    )
    value_gradient, column_states = lax.optimization_barrier((value_gradient, column_states))
    returned = exchange(ordered_dot(place.T, value_gradient))
    row_grads = ordered_dot(pack.T, returned)
    group_grads = lax.all_gather(row_grads, "fsdp", axis=0, tiled=True)
    term = lax.dot_general(
        column_states, group_grads, (((0,), (0,)), ((), ())), preferred_element_type=jnp.float32
    ).astype(low)
    score_scale = 1.0 / math.sqrt(token_count * device_count)
    dp = lax.axis_index("dp")
    rows = term.shape[0] // group_dp
    rings = [[(i, (i + step) % group_dp) for i in range(group_dp)] for step in range(group_dp)]
    summed = lax.dynamic_slice_in_dim(term, dp * rows, rows, 0).astype(jnp.float32)
    sent = []
    for step in range(1, group_dp):
        to = lax.rem(dp + step, group_dp)
        piece = lax.dynamic_slice_in_dim(term, to * rows, rows, 0)
        sent.append(lax.ppermute(piece, "dp", rings[step]))
    for piece in sent:
        summed = summed + piece.astype(jnp.float32)
    summed = summed.astype(low)
    weight_gradient = jnp.zeros(term.shape, jnp.float32)
    for step in range(group_dp):
        piece = lax.ppermute(summed, "dp", rings[step]) if step else summed
        source = lax.rem(dp + group_dp - step, group_dp)
        weight_gradient = lax.dynamic_update_slice_in_dim(
            weight_gradient, piece.astype(jnp.float32) * score_scale, source * rows, 0
        )
    return (attention_fn, query_gradient, key_gradient, weight_gradient)


def solution(mesh):
    in_specs = (
        P(("dp", "fsdp"), None),
        P(("dp", "fsdp"), None),
        P(("dp", "fsdp"), None),
        P(("dp", "fsdp")),
        P(("dp", "fsdp")),
        P(("dp", "fsdp")),
        P(("dp", "fsdp"), None),
        P("fsdp", None),
    )
    out_specs = (
        P(("dp", "fsdp"), None),
        P(("dp", "fsdp"), None),
        P(("dp", "fsdp"), None),
        P("fsdp", None),
    )
    return jax.shard_map(
        per_device, mesh=mesh, in_specs=in_specs, out_specs=out_specs, check_vma=False
    )
```

```python
import math

import jax
import jax.numpy as jnp
from jax import lax
from jax.experimental import pallas as pl
from jax.sharding import PartitionSpec as P

KEY_VALUE_HEADS = 8
HEAD_SIZE = 128
QUERY_HEADS = 32


def attend_kernel(q_ref, k_ref, v_ref, g_ref, col_ref, row_ref, o_ref, dq_ref, dk_ref, dv_ref):
    token_count = k_ref.shape[0]
    inverse = 1.0 / math.sqrt(HEAD_SIZE)
    low = q_ref.dtype
    query_at = lax.broadcasted_iota(jnp.int32, (token_count, token_count), 0)
    key_at = lax.broadcasted_iota(jnp.int32, (token_count, token_count), 1)
    allowed = (key_at <= query_at) & (row_ref[...] == col_ref[...])
    k = k_ref[...]
    v = v_ref[...]

    def dot(x, y, dims):
        return lax.dot_general(x, y, (dims, ((), ())), preferred_element_type=jnp.float32)

    for head in range(QUERY_HEADS // KEY_VALUE_HEADS):
        part = slice(head * HEAD_SIZE, (head + 1) * HEAD_SIZE)
        q = q_ref[:, part]
        g = g_ref[:, part]
        scores = jnp.where(allowed, dot(q, k, ((1,), (1,))) * inverse, -1e30)
        expon = jnp.exp(scores - jnp.max(scores, axis=1, keepdims=True))
        probs = expon * (1.0 / jnp.sum(expon, axis=1, keepdims=True))
        probs_low = probs.astype(low)
        o_ref[:, part] = dot(probs_low, v, ((1,), (0,))).astype(low)
        dprobs = dot(g, v, ((1,), (1,)))
        delta = jnp.sum(probs * dprobs, axis=1, keepdims=True)
        dscores = (probs * (dprobs - delta)).astype(low)
        dq_ref[:, part] = (dot(dscores, k, ((1,), (0,))) * inverse).astype(low)
        key_term = dot(dscores, q, ((0,), (0,)))
        value_term = dot(probs_low, g, ((0,), (0,)))
        dk = key_term if head == 0 else dk + key_term
        dv = value_term if head == 0 else dv + value_term
    dk_ref[...] = (dk * inverse).astype(low)
    dv_ref[...] = dv.astype(low)


def attend_block(q, k, v, segments, g):
    token_count = q.shape[0]
    wide = pl.BlockSpec((token_count, q.shape[1] // KEY_VALUE_HEADS), lambda h: (0, h))
    thin = pl.BlockSpec((token_count, HEAD_SIZE), lambda h: (0, h))
    col = pl.BlockSpec((token_count, 1), lambda h: (0, 0))
    row = pl.BlockSpec((1, token_count), lambda h: (0, 0))
    out = [jax.ShapeDtypeStruct(x.shape, q.dtype) for x in (q, q, k, k)]
    return pl.pallas_call(
        attend_kernel,
        grid=(KEY_VALUE_HEADS,),
        in_specs=[wide, thin, thin, wide, col, row],
        out_specs=[wide, wide, thin, thin],
        out_shape=out,
        cost_estimate=pl.CostEstimate(
            flops=12 * QUERY_HEADS * token_count * token_count * HEAD_SIZE,
            bytes_accessed=40 * token_count * QUERY_HEADS * HEAD_SIZE // 4,
            transcendentals=QUERY_HEADS * token_count * token_count,
        ),
    )(q, k, v, g, segments[:, None], segments[None, :])


def ordered_dot(one_hot, rows):
    return jnp.dot(one_hot, rows, preferred_element_type=jnp.float32).astype(rows.dtype)


def per_device(
    states, queries, keys, dest_device, dest_offset, response_numbers, cotangent, value_matrix
):
    token_count, model_width = states.shape
    group_dp = lax.axis_size("dp")
    group_fsdp = lax.axis_size("fsdp")
    device_count = group_dp * group_fsdp
    capacity = token_count // device_count
    everyone = ("dp", "fsdp")
    low = states.dtype
    block = model_width // group_fsdp
    me = lax.axis_index("fsdp")
    blocks = []
    for step in range(group_fsdp):
        to = lax.rem(me + step, group_fsdp)
        piece = lax.dynamic_slice_in_dim(states, to * block, block, 1)
        if step:
            pairs = [(i, (i + step) % group_fsdp) for i in range(group_fsdp)]
            piece = lax.ppermute(piece, "fsdp", pairs)
        blocks.append(piece)
    back = [blocks[-t % group_fsdp] for t in range(group_fsdp)]
    first = lax.rem(group_fsdp - me, group_fsdp) * token_count
    column_states = lax.dynamic_slice_in_dim(
        jnp.concatenate(back + back[:-1], axis=0), first, group_fsdp * token_count, 0
    )
    partial = jnp.dot(column_states, value_matrix, preferred_element_type=jnp.float32).astype(low)
    values = lax.psum_scatter(partial, "fsdp", scatter_dimension=0, tiled=True)

    row = jnp.arange(token_count, dtype=jnp.int32)
    earlier = (dest_device[:, None] == dest_device[None, :]) & (row[None, :] < row[:, None])
    slot = jnp.sum(earlier.astype(jnp.int32), axis=1)
    index = dest_device * capacity + slot
    pack = (index[None, :] == row[:, None]).astype(low)
    tail = jnp.broadcast_to(dest_offset.astype(low)[:, None], (token_count, 128))
    joined = jnp.concatenate([queries, keys, tail], axis=1)

    def exchange(rows):
        width = rows.shape[1]
        moved = lax.all_to_all(
            rows.reshape(device_count, capacity, width),
            everyone,
            split_axis=0,
            concat_axis=0,
            tiled=True,
        )
        return moved.reshape(token_count, width)

    got = exchange(ordered_dot(pack, joined))
    got_values = exchange(ordered_dot(pack, values))
    target = got[:, -128].astype(jnp.int32)
    place = (target[None, :] == row[:, None]).astype(low)
    query_width = queries.shape[1]
    placed = ordered_dot(place, got)
    learner_queries = placed[:, :query_width]
    learner_keys = placed[:, query_width : query_width + keys.shape[1]]
    attention_fn, query_gradient, key_gradient, value_gradient = attend_block(
        learner_queries, learner_keys, ordered_dot(place, got_values), response_numbers, cotangent
    )
    returned = exchange(ordered_dot(place.T, value_gradient))
    row_grads = ordered_dot(pack.T, returned)
    group_grads = lax.all_gather(row_grads, "fsdp", axis=0, tiled=True)
    term = lax.dot_general(
        column_states, group_grads, (((0,), (0,)), ((), ())), preferred_element_type=jnp.float32
    ).astype(low)
    score_scale = 1.0 / math.sqrt(token_count * device_count)
    dp = lax.axis_index("dp")
    rows = term.shape[0] // group_dp
    rings = [[(i, (i + step) % group_dp) for i in range(group_dp)] for step in range(group_dp)]
    summed = lax.dynamic_slice_in_dim(term, dp * rows, rows, 0).astype(jnp.float32)
    sent = []
    for step in range(1, group_dp):
        to = lax.rem(dp + step, group_dp)
        piece = lax.dynamic_slice_in_dim(term, to * rows, rows, 0)
        sent.append(lax.ppermute(piece, "dp", rings[step]))
    for piece in sent:
        summed = summed + piece.astype(jnp.float32)
    summed = summed.astype(low)
    weight_gradient = jnp.zeros(term.shape, jnp.float32)
    for step in range(group_dp):
        piece = lax.ppermute(summed, "dp", rings[step]) if step else summed
        source = lax.rem(dp + group_dp - step, group_dp)
        weight_gradient = lax.dynamic_update_slice_in_dim(
            weight_gradient, piece.astype(jnp.float32) * score_scale, source * rows, 0
        )
    return (attention_fn, query_gradient, key_gradient, weight_gradient)


def solution(mesh):
    in_specs = (
        P(("dp", "fsdp"), None),
        P(("dp", "fsdp"), None),
        P(("dp", "fsdp"), None),
        P(("dp", "fsdp")),
        P(("dp", "fsdp")),
        P(("dp", "fsdp")),
        P(("dp", "fsdp"), None),
        P("fsdp", None),
    )
    out_specs = (
        P(("dp", "fsdp"), None),
        P(("dp", "fsdp"), None),
        P(("dp", "fsdp"), None),
        P("fsdp", None),
    )
    return jax.shard_map(
        per_device, mesh=mesh, in_specs=in_specs, out_specs=out_specs, check_vma=False
    )
```
